512 devices in a mesh: span: 8 (over x, y_hi), seq: 64 (over y_lo, z, core).
Axes of the slice: x: 4, y: 4 (y_hi: 2, y_lo: 2; y = y_hi * 2 + y_lo), z: 16, core: 2. Of those that a mesh axis runs over, the one named last changes fastest.
Arguments:
- queries: bfloat16 [8, 512, 2560], P('span', 'seq'), may hold values from -8 to 8
- keys: bfloat16 [8, 512, 2560], P('span', 'seq'), may hold values from -8 to 8
- values: bfloat16 [8, 512, 2560], P('span', 'seq'), may hold values from -6 to 6
- span_index: int32 [8], replicated, may hold values from 0 to 7, each once
Outputs:
- attended: bfloat16 [8, 512, 2560], P('span', 'seq')
The draws below stay inside these ranges and needn't reach their ends.
Inputs may be any that keep to these rules, and one draw needn't show every extreme that they name: A permutation; group g denoises span span_index[g] and attends to itself and to the group holding the span before it.
All inputs are finite; a program needn't handle non-finite values.
Results may differ from the reference program's by a relative error of at most 0.015.
Values may be sent and summed in bfloat16 or wider, within the bound.
A program may use at most 64 MiB of HBM per device.

```python
import jax
import jax.numpy as jnp
from jax import lax

HEADS = 20
HD = 128
SPANS = 8
CLEN = 512


def draw_keys(key, part):
    key = jax.random.fold_in(key, 11)
    base = jnp.clip(jax.random.normal(key, (SPANS, CLEN, HEADS * HD), jnp.float32), -6.0, 6.0)
    return base.astype(jnp.bfloat16)


def draw_queries(key, part):
    key = jax.random.fold_in(key, 13)
    base = jnp.clip(jax.random.normal(key, (SPANS, CLEN, HEADS * HD), jnp.float32), -6.0, 6.0)
    return base.astype(jnp.bfloat16)


def shard_levels(rng, shape, shards, least, high):
    level = 1.0
    for dim, blocks in shards:
        heights = jax.random.uniform(jax.random.fold_in(jax.random.fold_in(rng, 6), dim), (blocks,), jnp.float32, least / len(shards), high / len(shards))
        level = level * jnp.repeat(jnp.exp(heights), shape[dim] // blocks).reshape((-1,) + (1,) * (len(shape) - 1 - dim))
    return level


def noise(key, extent, scale, reach, split=(), kind=jnp.bfloat16):
    values = scale * jax.random.normal(key, extent, jnp.float32)
    if split:
        values = values * shard_levels(key, extent, split, -0.22, 0.18)
    return jnp.clip(values, -reach, reach).astype(kind)


def setup_inputs(seed: int = 0) -> dict:
    key_of = jax.random.split(jax.random.key(seed), 5)
    queries = draw_queries(jax.random.fold_in(key_of[4], 71), 0)
    keys = draw_keys(jax.random.fold_in(key_of[4], 71), 0)
    values = noise(key_of[2], (SPANS, CLEN, HEADS * HD), 1.0, 6.0, ((0, 8), (1, 64)))
    span_index = jax.random.permutation(key_of[3], SPANS).astype(jnp.int32)
    return {"queries": queries, "keys": keys, "values": values, "span_index": span_index}


def reference(queries, keys, values, span_index):
    score_scale = HD ** -0.5
    group_ids = jnp.arange(SPANS, dtype=jnp.int32)
    results = []
    for group_pos in range(SPANS):
        my_span = span_index[group_pos]
        is_before = span_index == my_span - 1
        has_before = jnp.any(is_before)
        source_group = jnp.sum(jnp.where(is_before, group_ids, 0)).astype(jnp.int32)
        key_set = jnp.concatenate([keys[group_pos], keys[source_group]], 0).reshape(2 * CLEN, HEADS, HD)
        value_set = jnp.concatenate([values[group_pos], values[source_group]], 0).reshape(2 * CLEN, HEADS, HD)
        query_set = queries[group_pos].reshape(CLEN, HEADS, HD)
        scores = jnp.einsum("qhd,khd->hqk", query_set.astype(jnp.float32), key_set.astype(jnp.float32)) * score_scale
        key_mask = jnp.concatenate([jnp.ones((CLEN,), bool), jnp.full((CLEN,), has_before)])
        scores = jnp.where(key_mask, scores, -1e30)
        row_max = jnp.max(scores, axis=-1, keepdims=True)
        weights = jnp.where(key_mask, jnp.exp(scores - row_max), 0.0)
        weight_sum = jnp.sum(weights, axis=-1)
        rounded = lax.optimization_barrier(weights.astype(jnp.bfloat16)).astype(jnp.float32)
        accumulated = jnp.einsum("hqk,khd->hqd", rounded, value_set.astype(jnp.float32))
        result = (accumulated / weight_sum[..., None]).transpose(1, 0, 2).reshape(CLEN, HEADS * HD)
        results.append(result.astype(jnp.bfloat16))
    return jnp.stack(results)
```

```python
import functools

import jax
import jax.numpy as jnp
from jax import lax
from jax.experimental import pallas as pl
from jax.experimental.pallas import tpu as pltpu
from jax.sharding import PartitionSpec as P

HEADS = 20
HD = 128
GROUPS = 8
SEQ = 64
ROWS = 8
HALF = SEQ // 2
CHUNK = 128
SLOTS = CHUNK // ROWS
MESH = pl.DeviceIdType.MESH
F32 = jnp.float32
BF16 = jnp.bfloat16
SCALE = HD**-0.5


def seq_of(head):
    chip = (head * 8) // 5
    z, y = chip // 2, chip % 2
    y = (y + z // 8) % 2
    return y * HALF + z * 2


def head_of(seq):
    y, z, core = seq // HALF, (seq % HALF) // 2, seq % 2
    chip = z * 2 + (y + z // 8) % 2
    head = (chip * 5 + 7) // 8
    mine = jnp.logical_and((head * 8) // 5 == chip, core == 0)
    return jnp.minimum(head, HEADS - 1), mine


def dot(a, b, dims):
    return lax.dot_general(a, b, (dims, ((), ())), preferred_element_type=F32)


def kernel(
    span_ref, q_ref, k_ref, v_ref, out_ref,
    inbox, pack, spans, picked, own, prev, stats, acc, osend, ogot,
    in_sem, span_send, span_recv, own_send, own_recv, prev_send, prev_recv, out_send, out_recv,
):
    group = lax.axis_index("span")
    me = lax.axis_index("seq")
    head, is_head = head_of(me)

    loads = [
        pltpu.make_async_copy(ref.at[0], inbox.at[i], in_sem.at[i])
        for i, ref in enumerate((q_ref, k_ref, v_ref))
    ]
    for load in loads:
        load.start()

    def peer(step):
        other = (group + step) % GROUPS
        return other, (me + HALF * ((other + group) % 2)) % SEQ

    barrier = pltpu.get_barrier_semaphore()
    for step in range(1, GROUPS):
        pl.semaphore_signal(barrier, inc=1, device_id=peer(step), device_id_type=MESH)

    @pl.when(is_head)
    def _():
        @pl.loop(1, SEQ)
        def _(step):
            pl.semaphore_signal(barrier, inc=1, device_id=(group, (me + step) % SEQ), device_id_type=MESH)

    @pl.when(jnp.logical_not(is_head))
    def _():
        for h in range(HEADS):
            pl.semaphore_signal(barrier, inc=1, device_id=(group, seq_of(h)), device_id_type=MESH)

    for load in loads:
        load.wait()
    for h in range(HEADS):
        columns = slice(h * HD, (h + 1) * HD)
        for i in range(3):
            pack[h, i] = inbox[i, :, columns]
        for i in range(2):
            spans[group, h, i] = inbox[i + 1, :, columns]

    @pl.when(is_head)
    def _():
        pl.semaphore_wait(barrier, GROUPS - 1 + SEQ - 1)

    @pl.when(jnp.logical_not(is_head))
    def _():
        pl.semaphore_wait(barrier, GROUPS - 1 + HEADS)

    def span_copy(step):
        return pltpu.make_async_remote_copy(
            src_ref=spans.at[group],
            dst_ref=spans.at[group],
            send_sem=span_send,
            recv_sem=span_recv,
            device_id=peer(step),
            device_id_type=MESH,
        )

    def own_copy(h):
        return pltpu.make_async_remote_copy(
            src_ref=pack.at[h],
            dst_ref=own.at[me],
            send_sem=own_send,
            recv_sem=own_recv,
            device_id=(group, seq_of(h)),
            device_id_type=MESH,
        )

    def prev_copy(h):
        return pltpu.make_async_remote_copy(
            src_ref=picked.at[h],
            dst_ref=prev.at[me],
            send_sem=prev_send,
            recv_sem=prev_recv,
            device_id=(group, seq_of(h)),
            device_id_type=MESH,
        )

    for step in (1, 7, 2, 6, 3, 5, 4):
        span_copy(step).start()
    for h in range(HEADS):

        @pl.when(me != seq_of(h))
        def _(h=h):
            own_copy(h).start()

    @pl.when(is_head)
    def _():
        own[me] = pack[head]

    my_span = span_ref[group]
    source = jnp.int32(0)
    before = jnp.int32(0)
    for g in range(GROUPS):
        hit = span_ref[g] == my_span - 1
        source = jnp.where(hit, g, source)
        before = jnp.where(hit, 1, before)
    pltpu.make_async_copy(spans.at[pl.ds(0, GROUPS - 1)], spans.at[pl.ds(0, GROUPS - 1)], span_recv).wait()
    for h in range(HEADS):
        picked[h] = spans[source, h]

        @pl.when(me != seq_of(h))
        def _(h=h):
            prev_copy(h).start()

    @pl.when(is_head)
    def _():
        prev[me] = picked[head]
        whole = own.at[pl.ds(0, SEQ - 1)]
        pltpu.make_async_copy(whole, whole, own_recv).wait()
        keys = own[:, 1].reshape(SEQ * ROWS, HD)
        values = own[:, 2].reshape(SEQ * ROWS, HD)

        @pl.loop(0, SEQ // SLOTS)
        def _(c):
            rows = pl.ds(pl.multiple_of(c * CHUNK, CHUNK), CHUNK)
            queries = own[pl.ds(c * SLOTS, SLOTS), 0].reshape(CHUNK, HD)
            scores = dot(queries, keys, ((1,), (1,)))
            top = jnp.max(scores, axis=1, keepdims=True)
            weights = jnp.exp((scores - top) * SCALE)
            stats[0, rows] = jnp.broadcast_to(top, (CHUNK, HD))
            stats[1, rows] = jnp.broadcast_to(jnp.sum(weights, axis=1, keepdims=True), (CHUNK, HD))
            acc[rows] = dot(weights.astype(BF16), values, ((1,), (0,)))

        whole = prev.at[pl.ds(0, SEQ - 1)]
        pltpu.make_async_copy(whole, whole, prev_recv).wait()
        keys2 = prev[:, 0].reshape(SEQ * ROWS, HD)
        values2 = prev[:, 1].reshape(SEQ * ROWS, HD)

        @pl.loop(0, SEQ // SLOTS)
        def _(c):
            rows = pl.ds(pl.multiple_of(c * CHUNK, CHUNK), CHUNK)
            queries = own[pl.ds(c * SLOTS, SLOTS), 0].reshape(CHUNK, HD)
            scores = dot(queries, keys2, ((1,), (1,)))
            scores = jnp.where(before > 0, scores, -1e30)
            old = stats[0, rows][:, :1]
            top = jnp.maximum(old, jnp.max(scores, axis=1, keepdims=True))
            weights = jnp.exp((scores - top) * SCALE)
            fade = jnp.exp((old - top) * SCALE)
            total = stats[1, rows][:, :1] * fade + jnp.sum(weights, axis=1, keepdims=True)
            result = acc[rows] * fade + dot(weights.astype(BF16), values2, ((1,), (0,)))
            result = (result / total).reshape(SLOTS, ROWS, HD)
            osend[pl.ds(c * SLOTS, SLOTS)] = result.astype(BF16)
            for i in range(SLOTS):
                slot = c * SLOTS + i

                @pl.when(slot != me)
                def _():
                    pltpu.make_async_remote_copy(
                        src_ref=osend.at[slot],
                        dst_ref=ogot.at[head],
                        send_sem=out_send,
                        recv_sem=out_recv,
                        device_id=(group, slot),
                        device_id_type=MESH,
                    ).start()

        ogot[head] = osend[me]

    @pl.when(is_head)
    def _():
        whole = ogot.at[pl.ds(0, HEADS - 1)]
        pltpu.make_async_copy(whole, whole, out_recv).wait()

    @pl.when(jnp.logical_not(is_head))
    def _():
        pltpu.make_async_copy(ogot, ogot, out_recv).wait()

    for h in range(HEADS):
        out_ref[0, :, h * HD : (h + 1) * HD] = ogot[h]

    pltpu.make_async_copy(spans.at[pl.ds(0, GROUPS - 1)], spans.at[pl.ds(0, GROUPS - 1)], span_send).wait()

    @pl.when(is_head)
    def _():
        pltpu.make_async_copy(pack.at[pl.ds(0, HEADS - 1)], pack.at[pl.ds(0, HEADS - 1)], own_send).wait()
        pltpu.make_async_copy(picked.at[pl.ds(0, HEADS - 1)], picked.at[pl.ds(0, HEADS - 1)], prev_send).wait()
        pltpu.make_async_copy(osend.at[pl.ds(0, SEQ - 1)], osend.at[pl.ds(0, SEQ - 1)], out_send).wait()

    @pl.when(jnp.logical_not(is_head))
    def _():
        pltpu.make_async_copy(pack, pack, own_send).wait()
        pltpu.make_async_copy(picked, picked, prev_send).wait()


def solution(mesh):
    def shards(queries, keys, values, span_index):
        return pl.pallas_call(
            kernel,
            out_shape=jax.ShapeDtypeStruct((1, ROWS, HEADS * HD), BF16),
            in_specs=[pl.BlockSpec(memory_space=pltpu.SMEM)] + [pl.BlockSpec(memory_space=pl.ANY)] * 3,
            out_specs=pl.BlockSpec(memory_space=pltpu.VMEM),
            scratch_shapes=[
                pltpu.VMEM((3, ROWS, HEADS * HD), BF16),
                pltpu.VMEM((HEADS, 3, ROWS, HD), BF16),
                pltpu.VMEM((GROUPS, HEADS, 2, ROWS, HD), BF16),
                pltpu.VMEM((HEADS, 2, ROWS, HD), BF16),
                pltpu.VMEM((SEQ, 3, ROWS, HD), BF16),
                pltpu.VMEM((SEQ, 2, ROWS, HD), BF16),
                pltpu.VMEM((2, SEQ * ROWS, HD), F32),
                pltpu.VMEM((SEQ * ROWS, HD), F32),
                pltpu.VMEM((SEQ, ROWS, HD), BF16),
                pltpu.VMEM((HEADS, ROWS, HD), BF16),
                pltpu.SemaphoreType.DMA((3,)),
            ]
            + [pltpu.SemaphoreType.DMA] * 8,
            compiler_params=pltpu.CompilerParams(
                collective_id=0, has_side_effects=True, vmem_limit_bytes=32 * 1024 * 1024
            ),
        )(span_index, queries, keys, values)

    in_specs = (P("span", "seq", None), P("span", "seq", None), P("span", "seq", None), P())
    return jax.shard_map(shards, mesh=mesh, in_specs=in_specs, out_specs=P("span", "seq", None), check_vma=False)
```

```python
import functools

import jax
import jax.numpy as jnp
from jax import lax
from jax.experimental import pallas as pl
from jax.experimental.pallas import tpu as pltpu
from jax.sharding import PartitionSpec as P

HEADS = 20
HD = 128
GROUPS = 8
SEQ = 64
ROWS = 8
HALF = SEQ // 2
ZS = HALF // 2
CHUNK = 128
SLOTS = CHUNK // ROWS
MESH = pl.DeviceIdType.MESH
F32 = jnp.float32
BF16 = jnp.bfloat16
SCALE = HD**-0.5


HEAD_Z = (0, 1, 3, 4, 6, 8, 9, 11, 12, 14)
HEAD_SEQ = tuple(y * HALF + z * 2 for z in HEAD_Z for y in range(2))


def seq_of(head):
    if isinstance(head, int):
        return HEAD_SEQ[head]
    seq = jnp.int32(HEAD_SEQ[0])
    for h in range(1, HEADS):
        seq = jnp.where(head == h, HEAD_SEQ[h], seq)
    return seq


def head_of(seq):
    head = jnp.int32(0)
    mine = seq == HEAD_SEQ[0]
    for h in range(1, HEADS):
        head = jnp.where(seq == HEAD_SEQ[h], h, head)
        mine = jnp.logical_or(mine, seq == HEAD_SEQ[h])
    return head, mine


def part_of(head):
    return jnp.where(head < 2 * GROUPS, head // 2, 2 * (head - 2 * GROUPS))


def part_heads(part):
    return 2 * part, 2 * part + 1, 2 * GROUPS + part // 2


def send(kind, source, target, sems, device):
    pltpu.make_async_remote_copy(
        src_ref=source, dst_ref=target, send_sem=sems[0], recv_sem=sems[1], device_id=device, device_id_type=MESH
    ).start()


def wait(kind, ref, sem):
    pltpu.make_async_copy(ref, ref, sem).wait()


def dot(a, b, dims):
    return lax.dot_general(a, b, (dims, ((), ())), preferred_element_type=F32)


def kernel(
    span_ref, q_ref, k_ref, v_ref, out_ref,
    span, inbox, pack, parts, inter, picked, own, prev, stats, acc, osend, ogot,
    in_sem, span_sem, part_send, part_recv, own_send, own_recv, prev_send, prev_recv, out_send, out_recv,
):
    group = lax.axis_index("span")
    me = lax.axis_index("seq")
    core = me % 2
    head, is_head = head_of(me)
    z = (me % HALF) // 2
    part = (group + GROUPS - z % GROUPS) % GROUPS
    third = part % 2 == core
    to_self = jnp.logical_and(is_head, (part_of(head) + z) % GROUPS == group)

    def peer(step):
        other = (group + step) % GROUPS
        return other, (me + HALF * ((other + group) % 2)) % SEQ

    barrier = pltpu.get_barrier_semaphore()

    def greet(device):
        pl.semaphore_signal(barrier, inc=1, device_id=device, device_id_type=MESH)

    @pl.when(is_head)
    def _():
        for k in sorted(range(ZS), key=lambda k: -min(k, ZS - k)):
            for y in range(2):
                for c in range(2):
                    far = (z + k) % ZS
                    sender = y * HALF + 2 * far + c
                    via = (part_of(head) + jnp.where(head < 2 * GROUPS, 0, c) + far) % GROUPS
                    if k:
                        greet((group, sender))
                        greet((via, sender))
                    else:

                        @pl.when(sender != me)
                        def _():
                            greet((group, sender))

                        @pl.when(jnp.logical_or(via != group, sender != me))
                        def _():
                            greet((via, sender))

    @pl.when(jnp.logical_not(is_head))
    def _():
        for h in range(HEADS):
            greet((group, seq_of(h)))

    for step in range(1, GROUPS):
        greet(peer(step))

    loads = [pltpu.make_async_copy(span_ref, span, span_sem)] + [
        pltpu.make_async_copy(ref.at[0], inbox.at[i], in_sem.at[i])
        for i, ref in enumerate((q_ref, k_ref, v_ref))
    ]
    for load in loads:
        load.start()

    for load in loads:
        load.wait()
    for h in range(HEADS):
        columns = slice(h * HD, (h + 1) * HD)
        for i in range(3):
            pack[h, i] = inbox[i, :, columns]
    for p in range(GROUPS):
        for i, h in enumerate(part_heads(p)):
            for j in range(2):
                parts[p, i, j] = inbox[j + 1, :, h * HD : (h + 1) * HD]
    inter[group] = parts[part]

    spans = [span[g] for g in range(GROUPS)]
    sources = []
    for g in range(GROUPS):
        source = jnp.int32(0)
        for p in range(GROUPS):
            source = jnp.where(spans[p] == spans[g] - 1, p, source)
        sources.append(source)
    my_span = span[group]
    before = jnp.int32(0)
    for g in range(GROUPS):
        before = jnp.where(spans[g] == my_span - 1, 1, before)

    targets = [seq_of(h) for h in part_heads(part)]
    sent = 2 * GROUPS + jnp.where(third, GROUPS, 0) - jnp.where(to_self, 1, 0)
    greeted = GROUPS - 1 + jnp.where(is_head, SEQ - 1, HEADS) + sent
    pl.semaphore_wait(barrier, greeted)

    for step in (4, 3, 5, 2, 6, 1, 7):
        send("part", parts.at[(part + step) % GROUPS], inter.at[group], (part_send, part_recv), peer(step))
    for h in range(HEADS):

        @pl.when(me != seq_of(h))
        def _(h=h):
            send("own", pack.at[h], own.at[me], (own_send, own_recv), (group, seq_of(h)))

    @pl.when(is_head)
    def _():
        own[me] = pack[head]

    others = inter.at[pl.ds(0, GROUPS - 1)]
    wait("part", others, part_recv)

    def pass_on(g, i):
        target = targets[i]

        @pl.when(jnp.logical_or(group != g, me != target))
        def _():
            send("prev", picked.at[g, i], prev.at[me], (prev_send, prev_recv), (g, target))

        @pl.when(jnp.logical_and(group == g, me == target))
        def _():
            prev[me] = picked[g, i]

    for g in range(GROUPS):
        picked[g] = inter[sources[g]]
        for i in range(2):
            pass_on(g, i)

    @pl.when(third)
    def _():
        for g in range(GROUPS):
            pass_on(g, 2)

    @pl.when(is_head)
    def _():
        whole = own.at[pl.ds(0, SEQ - 1)]
        wait("own", whole, own_recv)
        keys = own[:, 1].reshape(SEQ * ROWS, HD)
        values = own[:, 2].reshape(SEQ * ROWS, HD)

        for c in (0, 2, 1, 3):
            rows = pl.ds(c * CHUNK, CHUNK)
            queries = own[pl.ds(c * SLOTS, SLOTS), 0].reshape(CHUNK, HD)
            scores = dot(queries, keys, ((1,), (1,)))
            top = jnp.max(scores, axis=1, keepdims=True)
            weights = jnp.exp((scores - top) * SCALE)
            stats[0, rows] = jnp.broadcast_to(top, (CHUNK, HD))
            stats[1, rows] = jnp.broadcast_to(jnp.sum(weights, axis=1, keepdims=True), (CHUNK, HD))
            acc[rows] = dot(weights.astype(BF16), values, ((1,), (0,)))

        @pl.when(to_self)
        def _():
            others = prev.at[pl.ds(0, SEQ - 1)]
            wait("prev", others, prev_recv)

        @pl.when(jnp.logical_not(to_self))
        def _():
            wait("prev", prev, prev_recv)

        keys2 = prev[:, 0].reshape(SEQ * ROWS, HD)
        values2 = prev[:, 1].reshape(SEQ * ROWS, HD)

        for c in (0, 2, 1, 3):
            rows = pl.ds(c * CHUNK, CHUNK)
            queries = own[pl.ds(c * SLOTS, SLOTS), 0].reshape(CHUNK, HD)
            scores = dot(queries, keys2, ((1,), (1,)))
            scores = jnp.where(before > 0, scores, -1e30)
            old = stats[0, rows][:, :1]
            top = jnp.maximum(old, jnp.max(scores, axis=1, keepdims=True))
            weights = jnp.exp((scores - top) * SCALE)
            fade = jnp.exp((old - top) * SCALE)
            total = stats[1, rows][:, :1] * fade + jnp.sum(weights, axis=1, keepdims=True)
            result = acc[rows] * fade + dot(weights.astype(BF16), values2, ((1,), (0,)))
            result = (result / total).reshape(SLOTS, ROWS, HD)
            osend[pl.ds(c * SLOTS, SLOTS)] = result.astype(BF16)
            for i in range(SLOTS):
                slot = c * SLOTS + i

                @pl.when(slot != me)
                def _(slot=slot):
                    send("out", osend.at[slot], ogot.at[head], (out_send, out_recv), (group, slot))

        ogot[head] = osend[me]

    @pl.when(is_head)
    def _():
        whole = ogot.at[pl.ds(0, HEADS - 1)]
        wait("out", whole, out_recv)

    @pl.when(jnp.logical_not(is_head))
    def _():
        wait("out", ogot, out_recv)

    for h in range(HEADS):
        out_ref[0, :, h * HD : (h + 1) * HD] = ogot[h]

    wait("part", others, part_send)

    @pl.when(is_head)
    def _():
        wait("own", pack.at[pl.ds(0, HEADS - 1)], own_send)
        wait("out", osend.at[pl.ds(0, SEQ - 1)], out_send)

    @pl.when(jnp.logical_not(is_head))
    def _():
        wait("own", pack, own_send)

    for count in (2 * GROUPS - 1, 2 * GROUPS, 3 * GROUPS - 1, 3 * GROUPS):

        @pl.when(sent == count)
        def _(count=count):
            left = prev.at[pl.ds(0, count)]
            wait("prev", left, prev_send)


def solution(mesh):
    def shards(queries, keys, values, span_index):
        return pl.pallas_call(
            kernel,
            out_shape=pltpu.VMEM((1, ROWS, HEADS * HD), BF16),
            in_specs=[pl.BlockSpec(memory_space=pl.ANY)] * 4,
            out_specs=pl.BlockSpec(memory_space=pltpu.VMEM),
            scratch_shapes=[
                pltpu.SMEM((GROUPS,), jnp.int32),
                pltpu.VMEM((3, ROWS, HEADS * HD), BF16),
                pltpu.VMEM((HEADS, 3, ROWS, HD), BF16),
                pltpu.VMEM((GROUPS, 3, 2, ROWS, HD), BF16),
                pltpu.VMEM((GROUPS, 3, 2, ROWS, HD), BF16),
                pltpu.VMEM((GROUPS, 3, 2, ROWS, HD), BF16),
                pltpu.VMEM((SEQ, 3, ROWS, HD), BF16),
                pltpu.VMEM((SEQ, 2, ROWS, HD), BF16),
                pltpu.VMEM((2, SEQ * ROWS, HD), F32),
                pltpu.VMEM((SEQ * ROWS, HD), F32),
                pltpu.VMEM((SEQ, ROWS, HD), BF16),
                pltpu.VMEM((HEADS, ROWS, HD), BF16),
                pltpu.SemaphoreType.DMA((3,)),
            ]
            + [pltpu.SemaphoreType.DMA] * 9,
            compiler_params=pltpu.CompilerParams(
                collective_id=0, has_side_effects=True, vmem_limit_bytes=60 * 1024 * 1024
            ),
        )(span_index, queries, keys, values)

    in_specs = (P("span", "seq", None), P("span", "seq", None), P("span", "seq", None), P())
    return jax.shard_map(shards, mesh=mesh, in_specs=in_specs, out_specs=P("span", "seq", None), check_vma=False)
```

```python
import functools

import jax
import jax.numpy as jnp
from jax import lax
from jax.experimental import pallas as pl
from jax.experimental.pallas import tpu as pltpu
from jax.sharding import PartitionSpec as P

HEADS = 20
HD = 128
GROUPS = 8
SEQ = 64
ROWS = 8
HALF = SEQ // 2
ZS = HALF // 2
CHUNK = 128
SLOTS = CHUNK // ROWS
MESH = pl.DeviceIdType.MESH
F32 = jnp.float32
BF16 = jnp.bfloat16
SCALE = HD**-0.5


HEAD_Z = (3, 4, 6, 8, 9, 11, 12, 14, 0, 1)
HEAD_SEQ = tuple(y * HALF + z * 2 for z in HEAD_Z for y in range(2))


def seq_of(head):
    if isinstance(head, int):
        return HEAD_SEQ[head]
    seq = jnp.int32(HEAD_SEQ[0])
    for h in range(1, HEADS):
        seq = jnp.where(head == h, HEAD_SEQ[h], seq)
    return seq


def head_of(seq):
    head = jnp.int32(0)
    mine = seq == HEAD_SEQ[0]
    for h in range(1, HEADS):
        head = jnp.where(seq == HEAD_SEQ[h], h, head)
        mine = jnp.logical_or(mine, seq == HEAD_SEQ[h])
    return head, mine


def part_of(head):
    return jnp.where(head < 2 * GROUPS, head // 2, 2 * (head - 2 * GROUPS))


def part_heads(part):
    return 2 * part, 2 * part + 1, 2 * GROUPS + part // 2


def send(kind, source, target, sems, device):
    pltpu.make_async_remote_copy(
        src_ref=source, dst_ref=target, send_sem=sems[0], recv_sem=sems[1], device_id=device, device_id_type=MESH
    ).start()


def wait(kind, ref, sem):
    pltpu.make_async_copy(ref, ref, sem).wait()


def dot(a, b, dims):
    return lax.dot_general(a, b, (dims, ((), ())), preferred_element_type=F32)


def kernel(
    span_ref, q_ref, k_ref, v_ref, out_ref,
    span, inbox, pack, parts, inter, picked, own, prev, stats, acc, osend, ogot,
    in_sem, span_sem, part_send, part_recv, own_send, own_recv, prev_send, prev_recv, out_send, out_recv, go,
):
    group = lax.axis_index("span")
    me = lax.axis_index("seq")
    core = me % 2
    head, is_head = head_of(me)
    z = (me % HALF) // 2
    part = (group + GROUPS - z % GROUPS) % GROUPS
    third = part % 2 == core
    to_self = jnp.logical_and(is_head, (part_of(head) + z) % GROUPS == group)

    def peer(step):
        other = (group + step) % GROUPS
        return other, (me + HALF * ((other + group) % 2)) % SEQ

    barrier = pltpu.get_barrier_semaphore()

    def greet(device):
        pl.semaphore_signal(barrier, inc=1, device_id=device, device_id_type=MESH)

    @pl.when(is_head)
    def _():
        for k in sorted(range(ZS), key=lambda k: -min(k, ZS - k)):
            for y in range(2):
                for c in range(2):
                    sender = y * HALF + 2 * ((z + k) % ZS) + c
                    if k:
                        greet((group, sender))
                    else:

                        @pl.when(sender != me)
                        def _():
                            greet((group, sender))

        for step in range(1, GROUPS, 2):
            greet(((group + step) % GROUPS, me))

    @pl.when(jnp.logical_not(is_head))
    def _():
        for h in range(HEADS):
            greet((group, seq_of(h)))

    for step in range(1, GROUPS):
        greet(peer(step))

    loads = [pltpu.make_async_copy(span_ref, span, span_sem)] + [
        pltpu.make_async_copy(ref.at[0], inbox.at[i], in_sem.at[i])
        for i, ref in enumerate((q_ref, k_ref, v_ref))
    ]
    for load in loads:
        load.start()

    for load in loads:
        load.wait()
    for h in range(HEADS):
        columns = slice(h * HD, (h + 1) * HD)
        for i in range(3):
            pack[h, i] = inbox[i, :, columns]
    for p in range(GROUPS):
        for i, h in enumerate(part_heads(p)):
            for j in range(2):
                parts[p, i, j] = inbox[j + 1, :, h * HD : (h + 1) * HD]
    inter[group] = parts[part]

    spans = [span[g] for g in range(GROUPS)]
    sources = []
    for step in range(GROUPS):
        wanted = span[(group + step) % GROUPS] - 1
        source = jnp.int32(0)
        for p in range(GROUPS):
            source = jnp.where(spans[p] == wanted, p, source)
        sources.append(source)
    my_span = span[group]
    before = jnp.int32(0)
    for g in range(GROUPS):
        before = jnp.where(spans[g] == my_span - 1, 1, before)

    targets = [seq_of(h) for h in part_heads(part)]
    sent = 2 * GROUPS + jnp.where(third, GROUPS, 0) - jnp.where(to_self, 1, 0)
    greeted = GROUPS - 1 + jnp.where(is_head, SEQ - 1 + GROUPS // 2, HEADS)
    pl.semaphore_wait(barrier, greeted)

    for step in (4, 3, 5, 2, 6, 1, 7):
        send("part", parts.at[(part + step) % GROUPS], inter.at[group], (part_send, part_recv), peer(step))
    @pl.when(is_head)
    def _():
        for c in range(2):
            low = (group + 2 * GROUPS - part_of(head) - jnp.where(head < 2 * GROUPS, 0, c)) % GROUPS
            for far in (low, low + GROUPS):
                for y in range(2):
                    passer = y * HALF + 2 * far + c

                    @pl.when(passer != me)
                    def _():
                        pl.semaphore_signal(go, inc=1, device_id=(group, passer), device_id_type=MESH)

    for h in range(HEADS):

        @pl.when(me != seq_of(h))
        def _(h=h):
            send("own", pack.at[h], own.at[me], (own_send, own_recv), (group, seq_of(h)))

    @pl.when(is_head)
    def _():
        own[me] = pack[head]

    others = inter.at[pl.ds(0, GROUPS - 1)]
    wait("part", others, part_recv)

    pl.semaphore_wait(go, 2 + jnp.where(third, 1, 0) - jnp.where(to_self, 1, 0))

    def pass_on(step, i):
        def copy():
            device = ((group + step) % GROUPS, targets[i])
            send("prev", picked.at[step, i], prev.at[me], (prev_send, prev_recv), device)

        if step:
            copy()
        else:
            pl.when(me != targets[i])(copy)

            @pl.when(me == targets[i])
            def _():
                prev[me] = picked[step, i]

    order = (5, 3, 4, 7, 1, 6, 2, 0)
    for step in order:
        picked[step] = inter[sources[step]]
        for i in range(2):
            pass_on(step, i)

    @pl.when(third)
    def _():
        for step in order:
            pass_on(step, 2)

    @pl.when(is_head)
    def _():
        whole = own.at[pl.ds(0, SEQ - 1)]
        wait("own", whole, own_recv)
        keys = own[:, 1].reshape(SEQ * ROWS, HD)
        values = own[:, 2].reshape(SEQ * ROWS, HD)

        def slots_of(c):
            return [pl.ds(y * HALF + c * SLOTS // 2, SLOTS // 2) for y in range(2)]

        def queries_of(c):
            return jnp.concatenate([own[slots, 0].reshape(CHUNK // 2, HD) for slots in slots_of(c)], 0)

        for c in range(SEQ // SLOTS):
            rows = pl.ds(c * CHUNK, CHUNK)
            queries = queries_of(c)
            scores = dot(queries, keys, ((1,), (1,)))
            top = jnp.max(scores, axis=1, keepdims=True)
            weights = jnp.exp((scores - top) * SCALE)
            stats[0, rows] = jnp.broadcast_to(top, (CHUNK, HD))
            stats[1, rows] = jnp.broadcast_to(jnp.sum(weights, axis=1, keepdims=True), (CHUNK, HD))
            acc[rows] = dot(weights.astype(BF16), values, ((1,), (0,)))

        @pl.when(to_self)
        def _():
            others = prev.at[pl.ds(0, SEQ - 1)]
            wait("prev", others, prev_recv)

        @pl.when(jnp.logical_not(to_self))
        def _():
            wait("prev", prev, prev_recv)

        keys2 = prev[:, 0].reshape(SEQ * ROWS, HD)
        values2 = prev[:, 1].reshape(SEQ * ROWS, HD)

        for c in range(SEQ // SLOTS):
            rows = pl.ds(c * CHUNK, CHUNK)
            queries = queries_of(c)
            scores = dot(queries, keys2, ((1,), (1,)))
            scores = jnp.where(before > 0, scores, -1e30)
            old = stats[0, rows][:, :1]
            top = jnp.maximum(old, jnp.max(scores, axis=1, keepdims=True))
            weights = jnp.exp((scores - top) * SCALE)
            fade = jnp.exp((old - top) * SCALE)
            total = stats[1, rows][:, :1] * fade + jnp.sum(weights, axis=1, keepdims=True)
            result = acc[rows] * fade + dot(weights.astype(BF16), values2, ((1,), (0,)))
            result = (result / total).reshape(2, SLOTS // 2, ROWS, HD).astype(BF16)
            for y, slots in enumerate(slots_of(c)):
                osend[slots] = result[y]
            for i in range(SLOTS):
                slot = (i % 2) * HALF + c * SLOTS // 2 + i // 2

                @pl.when(slot != me)
                def _(slot=slot):
                    send("out", osend.at[slot], ogot.at[head], (out_send, out_recv), (group, slot))

        ogot[head] = osend[me]

    @pl.when(is_head)
    def _():
        whole = ogot.at[pl.ds(0, HEADS - 1)]
        wait("out", whole, out_recv)

    @pl.when(jnp.logical_not(is_head))
    def _():
        wait("out", ogot, out_recv)

    for h in range(HEADS):
        out_ref[0, :, h * HD : (h + 1) * HD] = ogot[h]

    wait("part", others, part_send)

    @pl.when(is_head)
    def _():
        wait("own", pack.at[pl.ds(0, HEADS - 1)], own_send)
        wait("out", osend.at[pl.ds(0, SEQ - 1)], out_send)

    @pl.when(jnp.logical_not(is_head))
    def _():
        wait("own", pack, own_send)

    for count in (2 * GROUPS - 1, 2 * GROUPS, 3 * GROUPS - 1, 3 * GROUPS):

        @pl.when(sent == count)
        def _(count=count):
            left = prev.at[pl.ds(0, count)]
            wait("prev", left, prev_send)


def solution(mesh):
    def shards(queries, keys, values, span_index):
        return pl.pallas_call(
            kernel,
            out_shape=pltpu.VMEM((1, ROWS, HEADS * HD), BF16),
            in_specs=[pl.BlockSpec(memory_space=pl.ANY)] * 4,
            out_specs=pl.BlockSpec(memory_space=pltpu.VMEM),
            scratch_shapes=[
                pltpu.SMEM((GROUPS,), jnp.int32),
                pltpu.VMEM((3, ROWS, HEADS * HD), BF16),
                pltpu.VMEM((HEADS, 3, ROWS, HD), BF16),
                pltpu.VMEM((GROUPS, 3, 2, ROWS, HD), BF16),
                pltpu.VMEM((GROUPS, 3, 2, ROWS, HD), BF16),
                pltpu.VMEM((GROUPS, 3, 2, ROWS, HD), BF16),
                pltpu.VMEM((SEQ, 3, ROWS, HD), BF16),
                pltpu.VMEM((SEQ, 2, ROWS, HD), BF16),
                pltpu.VMEM((2, SEQ * ROWS, HD), F32),
                pltpu.VMEM((SEQ * ROWS, HD), F32),
                pltpu.VMEM((SEQ, ROWS, HD), BF16),
                pltpu.VMEM((HEADS, ROWS, HD), BF16),
                pltpu.SemaphoreType.DMA((3,)),
            ]
            + [pltpu.SemaphoreType.DMA] * 9
            + [pltpu.SemaphoreType.REGULAR],
            compiler_params=pltpu.CompilerParams(
                collective_id=0, has_side_effects=True, vmem_limit_bytes=60 * 1024 * 1024
            ),
        )(span_index, queries, keys, values)

    in_specs = (P("span", "seq", None), P("span", "seq", None), P("span", "seq", None), P())
    return jax.shard_map(shards, mesh=mesh, in_specs=in_specs, out_specs=P("span", "seq", None), check_vma=False)
```

```python
import functools

import jax
import jax.numpy as jnp
from jax import lax
from jax.experimental import pallas as pl
from jax.experimental.pallas import tpu as pltpu
from jax.sharding import PartitionSpec as P

HEADS = 20
HD = 128
GROUPS = 8
SEQ = 64
ROWS = 8
HALF = SEQ // 2
ZS = HALF // 2
CHUNK = 128
SLOTS = CHUNK // ROWS
MESH = pl.DeviceIdType.MESH
F32 = jnp.float32
BF16 = jnp.bfloat16
SCALE = HD**-0.5


HEAD_Z = (3, 4, 6, 8, 9, 11, 12, 14, 0, 1)
HEAD_SEQ = tuple(y * HALF + z * 2 for z in HEAD_Z for y in range(2))


NEAR_Z = 8
NEAR = tuple(seq % HALF < 2 * NEAR_Z for seq in HEAD_SEQ)


def near_of(head):
    near = jnp.bool_(NEAR[0])
    for h in range(1, HEADS):
        near = jnp.where(head == h, NEAR[h], near)
    return near


def seq_of(head):
    if isinstance(head, int):
        return HEAD_SEQ[head]
    seq = jnp.int32(HEAD_SEQ[0])
    for h in range(1, HEADS):
        seq = jnp.where(head == h, HEAD_SEQ[h], seq)
    return seq


def head_of(seq):
    head = jnp.int32(0)
    mine = seq == HEAD_SEQ[0]
    for h in range(1, HEADS):
        head = jnp.where(seq == HEAD_SEQ[h], h, head)
        mine = jnp.logical_or(mine, seq == HEAD_SEQ[h])
    return head, mine


def part_of(head):
    return jnp.where(head < 2 * GROUPS, head // 2, 2 * (head - 2 * GROUPS))


def part_heads(part):
    return 2 * part, 2 * part + 1, 2 * GROUPS + part // 2


def send(kind, source, target, sems, device):
    pltpu.make_async_remote_copy(
        src_ref=source, dst_ref=target, send_sem=sems[0], recv_sem=sems[1], device_id=device, device_id_type=MESH
    ).start()


def wait(kind, ref, sem):
    pltpu.make_async_copy(ref, ref, sem).wait()


def dot(a, b, dims):
    return lax.dot_general(a, b, (dims, ((), ())), preferred_element_type=F32)


def kernel(
    span_ref, q_ref, k_ref, v_ref, out_ref,
    span, inbox, pack, parts, inter, picked, own, prev, stats, acc, osend, ogot,
    in_sem, span_sem, part_send, part_recv, own_send, own_recv, prev_send, prev_recv, out_send, out_recv, go,
):
    group = lax.axis_index("span")
    me = lax.axis_index("seq")
    core = me % 2
    head, is_head = head_of(me)
    z = (me % HALF) // 2
    part = (group + GROUPS - z % GROUPS) % GROUPS
    third = part % 2 == core
    to_self = jnp.logical_and(is_head, (part_of(head) + z) % GROUPS == group)

    def peer(step):
        other = (group + step) % GROUPS
        return other, (me + HALF * ((other + group) % 2)) % SEQ

    barrier = pltpu.get_barrier_semaphore()

    def greet(device):
        pl.semaphore_signal(barrier, inc=1, device_id=device, device_id_type=MESH)

    @pl.when(is_head)
    def _():
        for k in sorted(range(ZS), key=lambda k: -min(k, ZS - k)):
            for y in range(2):
                for c in range(2):
                    sender = y * HALF + 2 * ((z + k) % ZS) + c
                    if k:
                        greet((group, sender))
                    else:

                        @pl.when(sender != me)
                        def _():
                            greet((group, sender))

        @pl.when(near_of(head))
        def _():
            for k in sorted(range(ZS), key=lambda k: -min(k, ZS - k)):
                far = (z + k) % ZS
                for y in range(2):
                    for c in range(2):
                        sender = y * HALF + 2 * far + c
                        via = (part_of(head) + jnp.where(head < 2 * GROUPS, 0, c) + far) % GROUPS

                        @pl.when(jnp.logical_or(via != group, sender != me))
                        def _():
                            greet((via, sender))

        for step in range(1, GROUPS, 2):
            greet(((group + step) % GROUPS, me))

    @pl.when(jnp.logical_not(is_head))
    def _():
        for h in sorted(range(HEADS), key=lambda h: HEAD_SEQ[h] % HALF):
            greet((group, seq_of(h)))

    for step in range(1, GROUPS):
        greet(peer(step))

    loads = [pltpu.make_async_copy(span_ref, span, span_sem)] + [
        pltpu.make_async_copy(ref.at[0], inbox.at[i], in_sem.at[i])
        for i, ref in enumerate((q_ref, k_ref, v_ref))
    ]
    for load in loads:
        load.start()

    for load in loads:
        load.wait()
    for h in range(HEADS):
        columns = slice(h * HD, (h + 1) * HD)
        for i in range(3):
            pack[h, i] = inbox[i, :, columns]
    for p in range(GROUPS):
        for i, h in enumerate(part_heads(p)):
            for j in range(2):
                parts[p, i, j] = inbox[j + 1, :, h * HD : (h + 1) * HD]
    inter[group] = parts[part]

    spans = [span[g] for g in range(GROUPS)]
    sources = []
    for g in range(GROUPS):
        source = jnp.int32(0)
        for p in range(GROUPS):
            source = jnp.where(spans[p] == spans[g] - 1, p, source)
        sources.append(source)
    my_span = span[group]
    before = jnp.int32(0)
    for g in range(GROUPS):
        before = jnp.where(spans[g] == my_span - 1, 1, before)

    targets = [seq_of(h) for h in part_heads(part)]
    sent = 2 * GROUPS + jnp.where(third, GROUPS, 0) - jnp.where(to_self, 1, 0)
    near_targets = [near_of(h) for h in part_heads(part)]
    near_sent = sum(jnp.where(near, GROUPS, 0) for near in near_targets[:2])
    near_sent += jnp.where(jnp.logical_and(third, near_targets[2]), GROUPS, 0)
    near_sent -= jnp.where(jnp.logical_and(to_self, near_of(head)), 1, 0)
    far_heads = sum(jnp.where(near, 0, 1) for near in near_targets[:2])
    far_heads += jnp.where(jnp.logical_and(third, jnp.logical_not(near_targets[2])), 1, 0)
    far_heads -= jnp.where(jnp.logical_and(to_self, jnp.logical_not(near_of(head))), 1, 0)
    greeted = near_sent + GROUPS - 1 + jnp.where(is_head, SEQ - 1 + GROUPS // 2, HEADS)
    pl.semaphore_wait(barrier, greeted)

    for step in (4, 3, 5, 2, 6, 1, 7):
        send("part", parts.at[(part + step) % GROUPS], inter.at[group], (part_send, part_recv), peer(step))
    @pl.when(jnp.logical_and(is_head, jnp.logical_not(near_of(head))))
    def _():
        for c in range(2):
            low = (group + 2 * GROUPS - part_of(head) - jnp.where(head < 2 * GROUPS, 0, c)) % GROUPS
            for far in (low, low + GROUPS):
                for y in range(2):
                    passer = y * HALF + 2 * far + c

                    @pl.when(passer != me)
                    def _():
                        pl.semaphore_signal(go, inc=1, device_id=(group, passer), device_id_type=MESH)

    farthest = ((z + 8 + ZS - 3) % ZS * 5) // 4
    for k in range(HEADS):
        h = (farthest + (k + 1) // 2 * (1 if k % 2 else -1) + HEADS) % HEADS
        target = seq_of(h)

        @pl.when(me != target)
        def _(h=h, target=target):
            send("own", pack.at[h], own.at[me], (own_send, own_recv), (group, target))

    @pl.when(is_head)
    def _():
        own[me] = pack[head]

    others = inter.at[pl.ds(0, GROUPS - 1)]
    wait("part", others, part_recv)

    @pl.when(far_heads > 0)
    def _():
        pl.semaphore_wait(go, far_heads)

    def pass_on(g, i):
        here = jnp.logical_and(group == g, me == targets[i])

        @pl.when(jnp.logical_not(here))
        def _():
            send("prev", picked.at[g, i], prev.at[me], (prev_send, prev_recv), (g, targets[i]))

        @pl.when(here)
        def _():
            prev[me] = picked[g, i]

    for g in (0, 4, 2, 6, 1, 5, 3, 7):
        picked[g] = inter[sources[g]]
        for i in range(2):
            pass_on(g, i)

        @pl.when(third)
        def _(g=g):
            pass_on(g, 2)

    @pl.when(is_head)
    def _():
        whole = own.at[pl.ds(0, SEQ - 1)]
        wait("own", whole, own_recv)
        keys = own[:, 1].reshape(SEQ * ROWS, HD)
        values = own[:, 2].reshape(SEQ * ROWS, HD)

        def slots_of(c):
            return [pl.ds(y * HALF + c * SLOTS // 2, SLOTS // 2) for y in range(2)]

        def queries_of(c):
            return jnp.concatenate([own[slots, 0].reshape(CHUNK // 2, HD) for slots in slots_of(c)], 0)

        for c in range(SEQ // SLOTS):
            rows = pl.ds(c * CHUNK, CHUNK)
            queries = queries_of(c)
            scores = dot(queries, keys, ((1,), (1,)))
            top = jnp.max(scores, axis=1, keepdims=True)
            weights = jnp.exp((scores - top) * SCALE)
            stats[0, rows] = jnp.broadcast_to(top, (CHUNK, HD))
            stats[1, rows] = jnp.broadcast_to(jnp.sum(weights, axis=1, keepdims=True), (CHUNK, HD))
            acc[rows] = dot(weights.astype(BF16), values, ((1,), (0,)))

        @pl.when(to_self)
        def _():
            others = prev.at[pl.ds(0, SEQ - 1)]
            wait("prev", others, prev_recv)

        @pl.when(jnp.logical_not(to_self))
        def _():
            wait("prev", prev, prev_recv)

        keys2 = prev[:, 0].reshape(SEQ * ROWS, HD)
        values2 = prev[:, 1].reshape(SEQ * ROWS, HD)

        for c in range(SEQ // SLOTS):
            rows = pl.ds(c * CHUNK, CHUNK)
            queries = queries_of(c)
            scores = dot(queries, keys2, ((1,), (1,)))
            scores = jnp.where(before > 0, scores, -1e30)
            old = stats[0, rows][:, :1]
            top = jnp.maximum(old, jnp.max(scores, axis=1, keepdims=True))
            weights = jnp.exp((scores - top) * SCALE)
            fade = jnp.exp((old - top) * SCALE)
            total = stats[1, rows][:, :1] * fade + jnp.sum(weights, axis=1, keepdims=True)
            result = acc[rows] * fade + dot(weights.astype(BF16), values2, ((1,), (0,)))
            result = (result / total).reshape(2, SLOTS // 2, ROWS, HD).astype(BF16)
            for y, slots in enumerate(slots_of(c)):
                osend[slots] = result[y]
            for i in range(SLOTS):
                slot = (i % 2) * HALF + c * SLOTS // 2 + i // 2

                @pl.when(slot != me)
                def _(slot=slot):
                    send("out", osend.at[slot], ogot.at[head], (out_send, out_recv), (group, slot))

        ogot[head] = osend[me]

    @pl.when(is_head)
    def _():
        whole = ogot.at[pl.ds(0, HEADS - 1)]
        wait("out", whole, out_recv)

    @pl.when(jnp.logical_not(is_head))
    def _():
        wait("out", ogot, out_recv)

    for h in range(HEADS):
        out_ref[0, :, h * HD : (h + 1) * HD] = ogot[h]

    wait("part", others, part_send)

    @pl.when(is_head)
    def _():
        wait("own", pack.at[pl.ds(0, HEADS - 1)], own_send)
        wait("out", osend.at[pl.ds(0, SEQ - 1)], out_send)

    @pl.when(jnp.logical_not(is_head))
    def _():
        wait("own", pack, own_send)

    for count in (2 * GROUPS - 1, 2 * GROUPS, 3 * GROUPS - 1, 3 * GROUPS):

        @pl.when(sent == count)
        def _(count=count):
            left = prev.at[pl.ds(0, count)]
            wait("prev", left, prev_send)


def solution(mesh):
    def shards(queries, keys, values, span_index):
        return pl.pallas_call(
            kernel,
            out_shape=pltpu.VMEM((1, ROWS, HEADS * HD), BF16),
            in_specs=[pl.BlockSpec(memory_space=pl.ANY)] * 4,
            out_specs=pl.BlockSpec(memory_space=pltpu.VMEM),
            scratch_shapes=[
                pltpu.SMEM((GROUPS,), jnp.int32),
                pltpu.VMEM((3, ROWS, HEADS * HD), BF16),
                pltpu.VMEM((HEADS, 3, ROWS, HD), BF16),
                pltpu.VMEM((GROUPS, 3, 2, ROWS, HD), BF16),
                pltpu.VMEM((GROUPS, 3, 2, ROWS, HD), BF16),
                pltpu.VMEM((GROUPS, 3, 2, ROWS, HD), BF16),
                pltpu.VMEM((SEQ, 3, ROWS, HD), BF16),
                pltpu.VMEM((SEQ, 2, ROWS, HD), BF16),
                pltpu.VMEM((2, SEQ * ROWS, HD), F32),
                pltpu.VMEM((SEQ * ROWS, HD), F32),
                pltpu.VMEM((SEQ, ROWS, HD), BF16),
                pltpu.VMEM((HEADS, ROWS, HD), BF16),
                pltpu.SemaphoreType.DMA((3,)),
            ]
            + [pltpu.SemaphoreType.DMA] * 9
            + [pltpu.SemaphoreType.REGULAR],
            compiler_params=pltpu.CompilerParams(
                collective_id=0, has_side_effects=True, vmem_limit_bytes=60 * 1024 * 1024
            ),
        )(span_index, queries, keys, values)

    in_specs = (P("span", "seq", None), P("span", "seq", None), P("span", "seq", None), P())
    return jax.shard_map(shards, mesh=mesh, in_specs=in_specs, out_specs=P("span", "seq", None), check_vma=False)
```

```python
import functools

import jax
import jax.numpy as jnp
from jax import lax
from jax.experimental import pallas as pl
from jax.experimental.pallas import tpu as pltpu
from jax.sharding import PartitionSpec as P

HEADS = 20
HD = 128
GROUPS = 8
SEQ = 64
ROWS = 8
HALF = SEQ // 2
ZS = HALF // 2
BANDS = ((0, 2), (2, 2), (4, 4), (8, 8))
MESH = pl.DeviceIdType.MESH
F32 = jnp.float32
BF16 = jnp.bfloat16
SCALE = HD**-0.5


HEAD_Z = (3, 4, 6, 8, 9, 11, 12, 14, 0, 1)
HEAD_SEQ = tuple(y * HALF + z * 2 for z in HEAD_Z for y in range(2))


NEAR_Z = 8
NEAR = tuple(seq % HALF < 2 * NEAR_Z for seq in HEAD_SEQ)


def near_of(head):
    near = jnp.bool_(NEAR[0])
    for h in range(1, HEADS):
        near = jnp.where(head == h, NEAR[h], near)
    return near


def seq_of(head):
    if isinstance(head, int):
        return HEAD_SEQ[head]
    seq = jnp.int32(HEAD_SEQ[0])
    for h in range(1, HEADS):
        seq = jnp.where(head == h, HEAD_SEQ[h], seq)
    return seq


def head_of(seq):
    head = jnp.int32(0)
    mine = seq == HEAD_SEQ[0]
    for h in range(1, HEADS):
        head = jnp.where(seq == HEAD_SEQ[h], h, head)
        mine = jnp.logical_or(mine, seq == HEAD_SEQ[h])
    return head, mine


def part_of(head):
    return jnp.where(head < 2 * GROUPS, head // 2, 2 * (head - 2 * GROUPS))


def part_heads(part):
    return 2 * part, 2 * part + 1, 2 * GROUPS + part // 2


def send(kind, source, target, sems, device):
    pltpu.make_async_remote_copy(
        src_ref=source, dst_ref=target, send_sem=sems[0], recv_sem=sems[1], device_id=device, device_id_type=MESH
    ).start()


def wait(kind, ref, sem):
    pltpu.make_async_copy(ref, ref, sem).wait()


def dot(a, b, dims):
    return lax.dot_general(a, b, (dims, ((), ())), preferred_element_type=F32)


def kernel(
    span_ref, q_ref, k_ref, v_ref, out_ref,
    span, inbox, pack, parts, inter, picked, own, prev, stats, acc, osend,
    in_sem, span_sem, part_send, part_recv, own_send, own_recv, prev_send, prev_recv, out_send, out_recv, go,
):
    group = lax.axis_index("span")
    me = lax.axis_index("seq")
    core = me % 2
    head, is_head = head_of(me)
    z = (me % HALF) // 2
    part = (group + GROUPS - z % GROUPS) % GROUPS
    third = part % 2 == core
    to_self = jnp.logical_and(is_head, (part_of(head) + z) % GROUPS == group)

    def peer(step):
        other = (group + step) % GROUPS
        return other, (me + HALF * ((other + group) % 2)) % SEQ

    barrier = pltpu.get_barrier_semaphore()

    def greet(device):
        pl.semaphore_signal(barrier, inc=1, device_id=device, device_id_type=MESH)

    @pl.when(is_head)
    def _():
        for k in sorted(range(ZS), key=lambda k: -min(k, ZS - k)):
            for y in range(2):
                for c in range(2):
                    sender = y * HALF + 2 * ((z + k) % ZS) + c
                    if k:
                        greet((group, sender))
                    else:

                        @pl.when(sender != me)
                        def _():
                            greet((group, sender))

        @pl.when(near_of(head))
        def _():
            for k in sorted(range(ZS), key=lambda k: -min(k, ZS - k)):
                far = (z + k) % ZS
                for y in range(2):
                    for c in range(2):
                        sender = y * HALF + 2 * far + c
                        via = (part_of(head) + jnp.where(head < 2 * GROUPS, 0, c) + far) % GROUPS

                        @pl.when(jnp.logical_or(via != group, sender != me))
                        def _():
                            greet((via, sender))

        for step in range(1, GROUPS, 2):
            greet(((group + step) % GROUPS, me))

    @pl.when(jnp.logical_not(is_head))
    def _():
        for h in sorted(range(HEADS), key=lambda h: HEAD_SEQ[h] % HALF):
            greet((group, seq_of(h)))

    for step in range(1, GROUPS):
        greet(peer(step))

    loads = [pltpu.make_async_copy(span_ref, span, span_sem)] + [
        pltpu.make_async_copy(ref.at[0], inbox.at[i], in_sem.at[i])
        for i, ref in enumerate((q_ref, k_ref, v_ref))
    ]
    for load in loads:
        load.start()

    for load in loads:
        load.wait()
    for h in range(HEADS):
        columns = slice(h * HD, (h + 1) * HD)
        for i in range(3):
            pack[h, i] = inbox[i, :, columns]
    for p in range(GROUPS):
        for i, h in enumerate(part_heads(p)):
            for j in range(2):
                parts[p, i, j] = inbox[j + 1, :, h * HD : (h + 1) * HD]
    inter[group] = parts[part]

    spans = [span[g] for g in range(GROUPS)]
    sources = []
    for g in range(GROUPS):
        source = jnp.int32(0)
        for p in range(GROUPS):
            source = jnp.where(spans[p] == spans[g] - 1, p, source)
        sources.append(source)
    my_span = span[group]
    before = jnp.int32(0)
    for g in range(GROUPS):
        before = jnp.where(spans[g] == my_span - 1, 1, before)

    targets = [seq_of(h) for h in part_heads(part)]
    sent = 2 * GROUPS + jnp.where(third, GROUPS, 0) - jnp.where(to_self, 1, 0)
    near_targets = [near_of(h) for h in part_heads(part)]
    near_sent = sum(jnp.where(near, GROUPS, 0) for near in near_targets[:2])
    near_sent += jnp.where(jnp.logical_and(third, near_targets[2]), GROUPS, 0)
    near_sent -= jnp.where(jnp.logical_and(to_self, near_of(head)), 1, 0)
    far_heads = sum(jnp.where(near, 0, 1) for near in near_targets[:2])
    far_heads += jnp.where(jnp.logical_and(third, jnp.logical_not(near_targets[2])), 1, 0)
    far_heads -= jnp.where(jnp.logical_and(to_self, jnp.logical_not(near_of(head))), 1, 0)
    greeted = near_sent + GROUPS - 1 + jnp.where(is_head, SEQ - 1 + GROUPS // 2, HEADS)
    pl.semaphore_wait(barrier, greeted)

    for step in (4, 3, 5, 2, 6, 1, 7):
        send("part", parts.at[(part + step) % GROUPS], inter.at[group], (part_send, part_recv), peer(step))
    @pl.when(jnp.logical_and(is_head, jnp.logical_not(near_of(head))))
    def _():
        for c in range(2):
            low = (group + 2 * GROUPS - part_of(head) - jnp.where(head < 2 * GROUPS, 0, c)) % GROUPS
            for far in (low, low + GROUPS):
                for y in range(2):
                    passer = y * HALF + 2 * far + c

                    @pl.when(passer != me)
                    def _():
                        pl.semaphore_signal(go, inc=1, device_id=(group, passer), device_id_type=MESH)

    farthest = ((z + 8 + ZS - 3) % ZS * 5) // 4
    for k in range(HEADS):
        h = (farthest + (k + 1) // 2 * (1 if k % 2 else -1) + HEADS) % HEADS
        target = seq_of(h)

        @pl.when(me != target)
        def _(h=h, target=target):
            send("own", pack.at[h], own.at[me], (own_send, own_recv), (group, target))

    @pl.when(is_head)
    def _():
        own[me] = pack[head]

    others = inter.at[pl.ds(0, GROUPS - 1)]
    wait("part", others, part_recv)

    @pl.when(far_heads > 0)
    def _():
        pl.semaphore_wait(go, far_heads)

    def pass_on(g, i):
        here = jnp.logical_and(group == g, me == targets[i])

        @pl.when(jnp.logical_not(here))
        def _():
            send("prev", picked.at[g, i], prev.at[me], (prev_send, prev_recv), (g, targets[i]))

        @pl.when(here)
        def _():
            prev[me] = picked[g, i]

    for g in (0, 4, 2, 6, 1, 5, 3, 7):
        picked[g] = inter[sources[g]]
        for i in range(2):
            pass_on(g, i)

        @pl.when(third)
        def _(g=g):
            pass_on(g, 2)

    @pl.when(is_head)
    def _():
        whole = own.at[pl.ds(0, SEQ - 1)]
        wait("own", whole, own_recv)
        keys = own[:, 1].reshape(SEQ * ROWS, HD)
        values = own[:, 2].reshape(SEQ * ROWS, HD)

        def slots_of(first, count):
            return [pl.ds(y * HALF + 2 * first, 2 * count) for y in range(2)]

        def rows_of(first, count):
            return pl.ds(4 * ROWS * first, 4 * ROWS * count)

        def queries_of(first, count):
            return jnp.concatenate([own[slots, 0].reshape(2 * ROWS * count, HD) for slots in slots_of(first, count)], 0)

        for first, count in BANDS:
            rows = rows_of(first, count)
            queries = queries_of(first, count)
            scores = dot(queries, keys, ((1,), (1,)))
            top = jnp.max(scores, axis=1, keepdims=True)
            weights = jnp.exp((scores - top) * SCALE)
            stats[0, rows] = jnp.broadcast_to(top, (4 * ROWS * count, HD))
            stats[1, rows] = jnp.broadcast_to(jnp.sum(weights, axis=1, keepdims=True), (4 * ROWS * count, HD))
            acc[rows] = dot(weights.astype(BF16), values, ((1,), (0,)))

        @pl.when(to_self)
        def _():
            others = prev.at[pl.ds(0, SEQ - 1)]
            wait("prev", others, prev_recv)

        @pl.when(jnp.logical_not(to_self))
        def _():
            wait("prev", prev, prev_recv)

        keys2 = prev[:, 0].reshape(SEQ * ROWS, HD)
        values2 = prev[:, 1].reshape(SEQ * ROWS, HD)

        columns = out_ref.at[0, :, pl.ds(pl.multiple_of(head * HD, HD), HD)]
        for first, count in BANDS:
            rows = rows_of(first, count)
            queries = queries_of(first, count)
            scores = dot(queries, keys2, ((1,), (1,)))
            scores = jnp.where(before > 0, scores, -1e30)
            old = stats[0, rows][:, :1]
            top = jnp.maximum(old, jnp.max(scores, axis=1, keepdims=True))
            weights = jnp.exp((scores - top) * SCALE)
            fade = jnp.exp((old - top) * SCALE)
            total = stats[1, rows][:, :1] * fade + jnp.sum(weights, axis=1, keepdims=True)
            result = acc[rows] * fade + dot(weights.astype(BF16), values2, ((1,), (0,)))
            result = (result * (1.0 / total)).reshape(2, 2 * count, ROWS, HD).astype(BF16)
            for y, slots in enumerate(slots_of(first, count)):
                osend[slots] = result[y]
            for i in range(4 * count):
                slot = i // 2 % 2 * HALF + 2 * (first + i // 4) + (i + 1) % 2

                @pl.when(slot != me)
                def _(slot=slot):
                    send("out", osend.at[slot], columns, (out_send, out_recv), (group, slot))

        out_ref[0, :, pl.ds(pl.multiple_of(head * HD, HD), HD)] = osend[me]

    @pl.when(is_head)
    def _():
        wait("out", out_ref.at[0, :, pl.ds(0, (HEADS - 1) * HD)], out_recv)

    @pl.when(jnp.logical_not(is_head))
    def _():
        wait("out", out_ref.at[0], out_recv)

    wait("part", others, part_send)

    @pl.when(is_head)
    def _():
        wait("own", pack.at[pl.ds(0, HEADS - 1)], own_send)
        wait("out", osend.at[pl.ds(0, SEQ - 1)], out_send)

    @pl.when(jnp.logical_not(is_head))
    def _():
        wait("own", pack, own_send)

    for count in (2 * GROUPS - 1, 2 * GROUPS, 3 * GROUPS - 1, 3 * GROUPS):

        @pl.when(sent == count)
        def _(count=count):
            left = prev.at[pl.ds(0, count)]
            wait("prev", left, prev_send)


def solution(mesh):
    def shards(queries, keys, values, span_index):
        return pl.pallas_call(
            kernel,
            out_shape=pltpu.VMEM((1, ROWS, HEADS * HD), BF16),
            in_specs=[pl.BlockSpec(memory_space=pl.ANY)] * 4,
            out_specs=pl.BlockSpec(memory_space=pltpu.VMEM),
            scratch_shapes=[
                pltpu.SMEM((GROUPS,), jnp.int32),
                pltpu.VMEM((3, ROWS, HEADS * HD), BF16),
                pltpu.VMEM((HEADS, 3, ROWS, HD), BF16),
                pltpu.VMEM((GROUPS, 3, 2, ROWS, HD), BF16),
                pltpu.VMEM((GROUPS, 3, 2, ROWS, HD), BF16),
                pltpu.VMEM((GROUPS, 3, 2, ROWS, HD), BF16),
                pltpu.VMEM((SEQ, 3, ROWS, HD), BF16),
                pltpu.VMEM((SEQ, 2, ROWS, HD), BF16),
                pltpu.VMEM((2, SEQ * ROWS, HD), F32),
                pltpu.VMEM((SEQ * ROWS, HD), F32),
                pltpu.VMEM((SEQ, ROWS, HD), BF16),
                pltpu.SemaphoreType.DMA((3,)),
            ]
            + [pltpu.SemaphoreType.DMA] * 9
            + [pltpu.SemaphoreType.REGULAR],
            compiler_params=pltpu.CompilerParams(
                collective_id=0, has_side_effects=True, vmem_limit_bytes=60 * 1024 * 1024
            ),
        )(span_index, queries, keys, values)

    in_specs = (P("span", "seq", None), P("span", "seq", None), P("span", "seq", None), P())
    return jax.shard_map(shards, mesh=mesh, in_specs=in_specs, out_specs=P("span", "seq", None), check_vma=False)
```

```python
import functools

import jax
import jax.numpy as jnp
from jax import lax
from jax.experimental import pallas as pl
from jax.experimental.pallas import tpu as pltpu
from jax.sharding import PartitionSpec as P

HEADS = 20
HD = 128
GROUPS = 8
SEQ = 64
ROWS = 8
HALF = SEQ // 2
ZS = HALF // 2
BANDS = ((0, 2), (2, 2), (4, 4), (8, 8))
MESH = pl.DeviceIdType.MESH
F32 = jnp.float32
BF16 = jnp.bfloat16
SCALE = HD**-0.5


HEAD_Z = (3, 4, 6, 7, 9, 11, 12, 14, 0, 1)
HEAD_SEQ = tuple(y * HALF + z * 2 for z in HEAD_Z for y in range(2))


NEAR_Z = 8
NEAR = tuple(seq % HALF < 2 * NEAR_Z for seq in HEAD_SEQ)


def near_of(head):
    near = jnp.bool_(NEAR[0])
    for h in range(1, HEADS):
        near = jnp.where(head == h, NEAR[h], near)
    return near


def seq_of(head):
    if isinstance(head, int):
        return HEAD_SEQ[head]
    seq = jnp.int32(HEAD_SEQ[0])
    for h in range(1, HEADS):
        seq = jnp.where(head == h, HEAD_SEQ[h], seq)
    return seq


def head_of(seq):
    head = jnp.int32(0)
    mine = seq == HEAD_SEQ[0]
    for h in range(1, HEADS):
        head = jnp.where(seq == HEAD_SEQ[h], h, head)
        mine = jnp.logical_or(mine, seq == HEAD_SEQ[h])
    return head, mine


def part_of(head):
    return jnp.where(head < 2 * GROUPS, head // 2, 2 * (head - 2 * GROUPS))


def part_heads(part):
    return 2 * part, 2 * part + 1, 2 * GROUPS + part // 2


def send(kind, source, target, sems, device):
    pltpu.make_async_remote_copy(
        src_ref=source, dst_ref=target, send_sem=sems[0], recv_sem=sems[1], device_id=device, device_id_type=MESH
    ).start()


def wait(kind, ref, sem):
    pltpu.make_async_copy(ref, ref, sem).wait()


def dot(a, b, dims):
    return lax.dot_general(a, b, (dims, ((), ())), preferred_element_type=F32)


def kernel(
    span_ref, q_ref, k_ref, v_ref, out_ref,
    span, inbox, pack, parts, inter, picked, own, prev, stats, acc, osend,
    in_sem, span_sem, part_send, part_recv, own_send, own_recv, prev_send, prev_recv, out_send, out_recv, go,
):
    group = lax.axis_index("span")
    me = lax.axis_index("seq")
    core = me % 2
    head, is_head = head_of(me)
    z = (me % HALF) // 2
    part = (group + GROUPS - z % GROUPS) % GROUPS
    third = part % 2 == core
    to_self = jnp.logical_and(is_head, (part_of(head) + z) % GROUPS == group)

    def peer(step):
        other = (group + step) % GROUPS
        return other, (me + HALF * ((other + group) % 2)) % SEQ

    barrier = pltpu.get_barrier_semaphore()

    def greet(device):
        pl.semaphore_signal(barrier, inc=1, device_id=device, device_id_type=MESH)

    @pl.when(is_head)
    def _():
        for k in sorted(range(ZS), key=lambda k: -min(k, ZS - k)):
            for y in range(2):
                for c in range(2):
                    sender = y * HALF + 2 * ((z + k) % ZS) + c
                    if k:
                        greet((group, sender))
                    else:

                        @pl.when(sender != me)
                        def _():
                            greet((group, sender))

        @pl.when(near_of(head))
        def _():
            for k in sorted(range(ZS), key=lambda k: -min(k, ZS - k)):
                far = (z + k) % ZS
                for y in range(2):
                    for c in range(2):
                        sender = y * HALF + 2 * far + c
                        via = (part_of(head) + jnp.where(head < 2 * GROUPS, 0, c) + far) % GROUPS

                        @pl.when(jnp.logical_or(via != group, sender != me))
                        def _():
                            greet((via, sender))

        for step in range(1, GROUPS, 2):
            greet(((group + step) % GROUPS, me))

    @pl.when(jnp.logical_not(is_head))
    def _():
        for h in sorted(range(HEADS), key=lambda h: HEAD_SEQ[h] % HALF):
            greet((group, seq_of(h)))

    for step in range(1, GROUPS):
        greet(peer(step))

    loads = [pltpu.make_async_copy(span_ref, span, span_sem)] + [
        pltpu.make_async_copy(ref.at[0], inbox.at[i], in_sem.at[i])
        for i, ref in enumerate((q_ref, k_ref, v_ref))
    ]
    for load in loads:
        load.start()

    for load in loads:
        load.wait()
    for h in range(HEADS):
        columns = slice(h * HD, (h + 1) * HD)
        for i in range(3):
            pack[h, i] = inbox[i, :, columns]
    for p in range(GROUPS):
        for i, h in enumerate(part_heads(p)):
            for j in range(2):
                parts[p, i, j] = inbox[j + 1, :, h * HD : (h + 1) * HD]
    inter[group] = parts[part]

    spans = [span[g] for g in range(GROUPS)]
    sources = []
    for g in range(GROUPS):
        source = jnp.int32(0)
        for p in range(GROUPS):
            source = jnp.where(spans[p] == spans[g] - 1, p, source)
        sources.append(source)
    my_span = span[group]
    before = jnp.int32(0)
    for g in range(GROUPS):
        before = jnp.where(spans[g] == my_span - 1, 1, before)

    targets = [seq_of(h) for h in part_heads(part)]
    sent = 2 * GROUPS + jnp.where(third, GROUPS, 0) - jnp.where(to_self, 1, 0)
    near_targets = [near_of(h) for h in part_heads(part)]
    near_sent = sum(jnp.where(near, GROUPS, 0) for near in near_targets[:2])
    near_sent += jnp.where(jnp.logical_and(third, near_targets[2]), GROUPS, 0)
    near_sent -= jnp.where(jnp.logical_and(to_self, near_of(head)), 1, 0)
    far_heads = sum(jnp.where(near, 0, 1) for near in near_targets[:2])
    far_heads += jnp.where(jnp.logical_and(third, jnp.logical_not(near_targets[2])), 1, 0)
    far_heads -= jnp.where(jnp.logical_and(to_self, jnp.logical_not(near_of(head))), 1, 0)
    greeted = near_sent + GROUPS - 1 + jnp.where(is_head, SEQ - 1 + GROUPS // 2, HEADS)
    pl.semaphore_wait(barrier, greeted)

    for step in (4, 3, 5, 2, 6, 1, 7):
        full = third if step % 2 == 0 else jnp.logical_not(third)

        @pl.when(full)
        def _(step=step):
            send("part", parts.at[(part + step) % GROUPS], inter.at[group], (part_send, part_recv), peer(step))

        @pl.when(jnp.logical_not(full))
        def _(step=step):
            two = pl.ds(0, 2)
            source, target = parts.at[(part + step) % GROUPS, two], inter.at[group, two]
            send("part", source, target, (part_send, part_recv), peer(step))

    @pl.when(jnp.logical_and(is_head, jnp.logical_not(near_of(head))))
    def _():
        for c in range(2):
            low = (group + 2 * GROUPS - part_of(head) - jnp.where(head < 2 * GROUPS, 0, c)) % GROUPS
            for far in (low, low + GROUPS):
                for y in range(2):
                    passer = y * HALF + 2 * far + c

                    @pl.when(passer != me)
                    def _():
                        pl.semaphore_signal(go, inc=1, device_id=(group, passer), device_id_type=MESH)

    farthest = ((z + ZS - 3) % ZS * 5) // 4
    for k in range(HEADS):
        h = (farthest + (k + 1) // 2 * (1 if k % 2 else -1) + HEADS) % HEADS
        target = seq_of(h)

        @pl.when(me != target)
        def _(h=h, target=target):
            send("own", pack.at[h], own.at[me], (own_send, own_recv), (group, target))

    @pl.when(is_head)
    def _():
        own[me] = pack[head]

    @pl.when(third)
    def _():
        wait("part", inter.at[pl.ds(0, GROUPS - 1)], part_recv)

    @pl.when(jnp.logical_not(third))
    def _():
        wait("part", inter.at[pl.ds(0, GROUPS - 1), pl.ds(0, 2)], part_recv)

    @pl.when(far_heads > 0)
    def _():
        pl.semaphore_wait(go, far_heads)

    def pass_on(g, i):
        here = jnp.logical_and(group == g, me == targets[i])

        @pl.when(jnp.logical_not(here))
        def _():
            send("prev", picked.at[g, i], prev.at[me], (prev_send, prev_recv), (g, targets[i]))

        @pl.when(here)
        def _():
            prev[me] = picked[g, i]

    for g in (0, 4, 2, 6, 1, 5, 3, 7):
        picked[g, pl.ds(0, 2)] = inter[sources[g], pl.ds(0, 2)]
        for i in range(2):
            pass_on(g, i)

    @pl.when(third)
    def _():
        for g in (0, 4, 2, 6, 1, 5, 3, 7):
            picked[g, 2] = inter[sources[g], 2]
            pass_on(g, 2)

    @pl.when(is_head)
    def _():
        whole = own.at[pl.ds(0, SEQ - 1)]
        wait("own", whole, own_recv)
        keys = own[:, 1].reshape(SEQ * ROWS, HD)
        values = own[:, 2].reshape(SEQ * ROWS, HD)

        def slots_of(first, count):
            return [pl.ds(y * HALF + 2 * first, 2 * count) for y in range(2)]

        def rows_of(first, count):
            return pl.ds(4 * ROWS * first, 4 * ROWS * count)

        def queries_of(first, count):
            return jnp.concatenate([own[slots, 0].reshape(2 * ROWS * count, HD) for slots in slots_of(first, count)], 0)

        for first, count in BANDS:
            rows = rows_of(first, count)
            queries = queries_of(first, count)
            scores = dot(queries, keys, ((1,), (1,)))
            top = jnp.max(scores, axis=1, keepdims=True)
            weights = jnp.exp((scores - top) * SCALE)
            stats[0, rows] = jnp.broadcast_to(top, (4 * ROWS * count, HD))
            stats[1, rows] = jnp.broadcast_to(jnp.sum(weights, axis=1, keepdims=True), (4 * ROWS * count, HD))
            acc[rows] = dot(weights.astype(BF16), values, ((1,), (0,)))

        @pl.when(to_self)
        def _():
            others = prev.at[pl.ds(0, SEQ - 1)]
            wait("prev", others, prev_recv)

        @pl.when(jnp.logical_not(to_self))
        def _():
            wait("prev", prev, prev_recv)

        keys2 = prev[:, 0].reshape(SEQ * ROWS, HD)
        values2 = prev[:, 1].reshape(SEQ * ROWS, HD)

        columns = out_ref.at[0, :, pl.ds(pl.multiple_of(head * HD, HD), HD)]
        for first, count in BANDS:
            rows = rows_of(first, count)
            queries = queries_of(first, count)
            scores = dot(queries, keys2, ((1,), (1,)))
            scores = jnp.where(before > 0, scores, -1e30)
            old = stats[0, rows][:, :1]
            top = jnp.maximum(old, jnp.max(scores, axis=1, keepdims=True))
            weights = jnp.exp((scores - top) * SCALE)
            fade = jnp.exp((old - top) * SCALE)
            total = stats[1, rows][:, :1] * fade + jnp.sum(weights, axis=1, keepdims=True)
            result = acc[rows] * fade + dot(weights.astype(BF16), values2, ((1,), (0,)))
            result = (result * (1.0 / total)).reshape(2, 2 * count, ROWS, HD).astype(BF16)
            for y, slots in enumerate(slots_of(first, count)):
                osend[slots] = result[y]
            for i in range(4 * count):
                slot = i // 2 % 2 * HALF + 2 * (first + i // 4) + (i + 1) % 2

                @pl.when(slot != me)
                def _(slot=slot):
                    send("out", osend.at[slot], columns, (out_send, out_recv), (group, slot))

        out_ref[0, :, pl.ds(pl.multiple_of(head * HD, HD), HD)] = osend[me]

    @pl.when(is_head)
    def _():
        wait("out", out_ref.at[0, :, pl.ds(0, (HEADS - 1) * HD)], out_recv)

    @pl.when(jnp.logical_not(is_head))
    def _():
        wait("out", out_ref.at[0], out_recv)

    @pl.when(third)
    def _():
        wait("part", prev.at[pl.ds(0, 3 * 3 + 4 * 2)], part_send)

    @pl.when(jnp.logical_not(third))
    def _():
        wait("part", prev.at[pl.ds(0, 3 * 2 + 4 * 3)], part_send)

    @pl.when(is_head)
    def _():
        wait("own", pack.at[pl.ds(0, HEADS - 1)], own_send)
        wait("out", osend.at[pl.ds(0, SEQ - 1)], out_send)

    @pl.when(jnp.logical_not(is_head))
    def _():
        wait("own", pack, own_send)

    for count in (2 * GROUPS - 1, 2 * GROUPS, 3 * GROUPS - 1, 3 * GROUPS):

        @pl.when(sent == count)
        def _(count=count):
            left = prev.at[pl.ds(0, count)]
            wait("prev", left, prev_send)


def solution(mesh):
    def shards(queries, keys, values, span_index):
        return pl.pallas_call(
            kernel,
            out_shape=pltpu.VMEM((1, ROWS, HEADS * HD), BF16),
            in_specs=[pl.BlockSpec(memory_space=pl.ANY)] * 4,
            out_specs=pl.BlockSpec(memory_space=pltpu.VMEM),
            scratch_shapes=[
                pltpu.SMEM((GROUPS,), jnp.int32),
                pltpu.VMEM((3, ROWS, HEADS * HD), BF16),
                pltpu.VMEM((HEADS, 3, ROWS, HD), BF16),
                pltpu.VMEM((GROUPS, 3, 2, ROWS, HD), BF16),
                pltpu.VMEM((GROUPS, 3, 2, ROWS, HD), BF16),
                pltpu.VMEM((GROUPS, 3, 2, ROWS, HD), BF16),
                pltpu.VMEM((SEQ, 3, ROWS, HD), BF16),
                pltpu.VMEM((SEQ, 2, ROWS, HD), BF16),
                pltpu.VMEM((2, SEQ * ROWS, HD), F32),
                pltpu.VMEM((SEQ * ROWS, HD), F32),
                pltpu.VMEM((SEQ, ROWS, HD), BF16),
                pltpu.SemaphoreType.DMA((3,)),
            ]
            + [pltpu.SemaphoreType.DMA] * 9
            + [pltpu.SemaphoreType.REGULAR],
            compiler_params=pltpu.CompilerParams(
                collective_id=0, has_side_effects=True, vmem_limit_bytes=60 * 1024 * 1024
            ),
        )(span_index, queries, keys, values)

    in_specs = (P("span", "seq", None), P("span", "seq", None), P("span", "seq", None), P())
    return jax.shard_map(shards, mesh=mesh, in_specs=in_specs, out_specs=P("span", "seq", None), check_vma=False)
```

```python
import functools

import jax
import jax.numpy as jnp
from jax import lax
from jax.experimental import pallas as pl
from jax.experimental.pallas import tpu as pltpu
from jax.sharding import PartitionSpec as P

HEADS = 20
HD = 128
GROUPS = 8
SEQ = 64
ROWS = 8
HALF = SEQ // 2
ZS = HALF // 2
BANDS = ((0, 2), (2, 2), (4, 4), (8, 8))
MESH = pl.DeviceIdType.MESH
F32 = jnp.float32
BF16 = jnp.bfloat16
SCALE = HD**-0.5


HEAD_Z = (3, 4, 6, 8, 9, 11, 12, 14, 0, 1)
HEAD_SEQ = tuple(y * HALF + z * 2 for z in HEAD_Z for y in range(2))


NEAR_Z = 8
NEAR = tuple(seq % HALF < 2 * NEAR_Z for seq in HEAD_SEQ)


def near_of(head):
    near = jnp.bool_(NEAR[0])
    for h in range(1, HEADS):
        near = jnp.where(head == h, NEAR[h], near)
    return near


def seq_of(head):
    if isinstance(head, int):
        return HEAD_SEQ[head]
    seq = jnp.int32(HEAD_SEQ[0])
    for h in range(1, HEADS):
        seq = jnp.where(head == h, HEAD_SEQ[h], seq)
    return seq


def head_of(seq):
    head = jnp.int32(0)
    mine = seq == HEAD_SEQ[0]
    for h in range(1, HEADS):
        head = jnp.where(seq == HEAD_SEQ[h], h, head)
        mine = jnp.logical_or(mine, seq == HEAD_SEQ[h])
    return head, mine


def part_of(head):
    return jnp.where(head < 2 * GROUPS, head // 2, 2 * (head - 2 * GROUPS))


def part_heads(part):
    return 2 * part, 2 * part + 1, 2 * GROUPS + part // 2


def send(kind, source, target, sems, device):
    pltpu.make_async_remote_copy(
        src_ref=source, dst_ref=target, send_sem=sems[0], recv_sem=sems[1], device_id=device, device_id_type=MESH
    ).start()


def wait(kind, ref, sem):
    pltpu.make_async_copy(ref, ref, sem).wait()


def dot(a, b, dims):
    return lax.dot_general(a, b, (dims, ((), ())), preferred_element_type=F32)


def kernel(
    span_ref, q_ref, k_ref, v_ref, out_ref,
    span, inbox, pack, parts, inter, picked, own, prev, stats, acc, osend,
    in_sem, span_sem, part_send, part_recv, own_send, own_recv, prev_send, prev_recv, out_send, out_recv, go,
):
    group = lax.axis_index("span")
    me = lax.axis_index("seq")
    core = me % 2
    head, is_head = head_of(me)
    z = (me % HALF) // 2
    part = (group + GROUPS - z % GROUPS) % GROUPS
    third = part % 2 == core
    to_self = jnp.logical_and(is_head, (part_of(head) + z) % GROUPS == group)

    def peer(step):
        other = (group + step) % GROUPS
        return other, (me + HALF * ((other + group) % 2)) % SEQ

    barrier = pltpu.get_barrier_semaphore()

    def greet(device):
        pl.semaphore_signal(barrier, inc=1, device_id=device, device_id_type=MESH)

    @pl.when(is_head)
    def _():
        for k in sorted(range(ZS), key=lambda k: -min(k, ZS - k)):
            for y in range(2):
                for c in range(2):
                    sender = y * HALF + 2 * ((z + k) % ZS) + c
                    if k:
                        greet((group, sender))
                    else:

                        @pl.when(sender != me)
                        def _():
                            greet((group, sender))

        @pl.when(near_of(head))
        def _():
            for k in sorted(range(ZS), key=lambda k: -min(k, ZS - k)):
                far = (z + k) % ZS
                for y in range(2):
                    for c in range(2):
                        sender = y * HALF + 2 * far + c
                        via = (part_of(head) + jnp.where(head < 2 * GROUPS, 0, c) + far) % GROUPS

                        @pl.when(jnp.logical_or(via != group, sender != me))
                        def _():
                            greet((via, sender))

        for step in range(1, GROUPS, 2):
            greet(((group + step) % GROUPS, me))

    @pl.when(jnp.logical_not(is_head))
    def _():
        for h in sorted(range(HEADS), key=lambda h: HEAD_SEQ[h] % HALF):
            greet((group, seq_of(h)))

    for step in range(1, GROUPS):
        greet(peer(step))

    loads = [pltpu.make_async_copy(span_ref, span, span_sem)] + [
        pltpu.make_async_copy(ref.at[0], inbox.at[i], in_sem.at[i])
        for i, ref in enumerate((q_ref, k_ref, v_ref))
    ]
    for load in loads:
        load.start()

    for load in loads:
        load.wait()
    for h in range(HEADS):
        columns = slice(h * HD, (h + 1) * HD)
        for i in range(3):
            pack[h, i] = inbox[i, :, columns]
    for p in range(GROUPS):
        for i, h in enumerate(part_heads(p)):
            for j in range(2):
                parts[p, i, j] = inbox[j + 1, :, h * HD : (h + 1) * HD]
    inter[group] = parts[part]

    spans = [span[g] for g in range(GROUPS)]
    sources = []
    for g in range(GROUPS):
        source = jnp.int32(0)
        for p in range(GROUPS):
            source = jnp.where(spans[p] == spans[g] - 1, p, source)
        sources.append(source)
    my_span = span[group]
    before = jnp.int32(0)
    for g in range(GROUPS):
        before = jnp.where(spans[g] == my_span - 1, 1, before)

    targets = [seq_of(h) for h in part_heads(part)]
    sent = 2 * GROUPS + jnp.where(third, GROUPS, 0) - jnp.where(to_self, 1, 0)
    near_targets = [near_of(h) for h in part_heads(part)]
    near_sent = sum(jnp.where(near, GROUPS, 0) for near in near_targets[:2])
    near_sent += jnp.where(jnp.logical_and(third, near_targets[2]), GROUPS, 0)
    near_sent -= jnp.where(jnp.logical_and(to_self, near_of(head)), 1, 0)
    far_heads = sum(jnp.where(near, 0, 1) for near in near_targets[:2])
    far_heads += jnp.where(jnp.logical_and(third, jnp.logical_not(near_targets[2])), 1, 0)
    far_heads -= jnp.where(jnp.logical_and(to_self, jnp.logical_not(near_of(head))), 1, 0)
    greeted = near_sent + GROUPS - 1 + jnp.where(is_head, SEQ - 1 + GROUPS // 2, HEADS)
    pl.semaphore_wait(barrier, greeted)

    for step in (4, 3, 5, 2, 6, 1, 7):
        send("part", parts.at[(part + step) % GROUPS], inter.at[group], (part_send, part_recv), peer(step))
    @pl.when(jnp.logical_and(is_head, jnp.logical_not(near_of(head))))
    def _():
        for c in range(2):
            low = (group + 2 * GROUPS - part_of(head) - jnp.where(head < 2 * GROUPS, 0, c)) % GROUPS
            for far in (low, low + GROUPS):
                for y in range(2):
                    passer = y * HALF + 2 * far + c

                    @pl.when(passer != me)
                    def _():
                        pl.semaphore_signal(go, inc=1, device_id=(group, passer), device_id_type=MESH)

    farthest = ((z + 8 + ZS - 3) % ZS * 5) // 4
    for k in range(HEADS):
        h = (farthest + (k + 1) // 2 * (1 if k % 2 else -1) + HEADS) % HEADS
        target = seq_of(h)

        @pl.when(me != target)
        def _(h=h, target=target):
            send("own", pack.at[h], own.at[me], (own_send, own_recv), (group, target))

    @pl.when(is_head)
    def _():
        own[me] = pack[head]

    others = inter.at[pl.ds(0, GROUPS - 1)]
    wait("part", others, part_recv)

    @pl.when(far_heads > 0)
    def _():
        pl.semaphore_wait(go, far_heads)

    def pass_on(g, i):
        here = jnp.logical_and(group == g, me == targets[i])

        @pl.when(jnp.logical_not(here))
        def _():
            send("prev", picked.at[g, i], prev.at[me], (prev_send, prev_recv), (g, targets[i]))

    for g in (0, 4, 2, 6, 1, 5, 3, 7):
        picked[g] = inter[sources[g]]
        for i in range(2):
            pass_on(g, i)

        @pl.when(third)
        def _(g=g):
            pass_on(g, 2)

    @pl.when(to_self)
    def _():
        prev[me] = picked[group, jnp.where(head < 2 * GROUPS, head % 2, 2)]

    @pl.when(is_head)
    def _():
        whole = own.at[pl.ds(0, SEQ - 1)]
        wait("own", whole, own_recv)
        keys = own[:, 1].reshape(SEQ * ROWS, HD)
        values = own[:, 2].reshape(SEQ * ROWS, HD)

        def slots_of(first, count):
            return [pl.ds(y * HALF + 2 * first, 2 * count) for y in range(2)]

        def rows_of(first, count):
            return pl.ds(4 * ROWS * first, 4 * ROWS * count)

        def queries_of(first, count):
            return jnp.concatenate([own[slots, 0].reshape(2 * ROWS * count, HD) for slots in slots_of(first, count)], 0)

        for first, count in BANDS:
            rows = rows_of(first, count)
            queries = queries_of(first, count)
            scores = dot(queries, keys, ((1,), (1,)))
            top = jnp.max(scores, axis=1, keepdims=True)
            weights = jnp.exp((scores - top) * SCALE)
            stats[0, rows] = jnp.broadcast_to(top, (4 * ROWS * count, HD))
            stats[1, rows] = jnp.broadcast_to(jnp.sum(weights, axis=1, keepdims=True), (4 * ROWS * count, HD))
            acc[rows] = dot(weights.astype(BF16), values, ((1,), (0,)))

        @pl.when(to_self)
        def _():
            others = prev.at[pl.ds(0, SEQ - 1)]
            wait("prev", others, prev_recv)

        @pl.when(jnp.logical_not(to_self))
        def _():
            wait("prev", prev, prev_recv)

        keys2 = prev[:, 0].reshape(SEQ * ROWS, HD)
        values2 = prev[:, 1].reshape(SEQ * ROWS, HD)

        columns = out_ref.at[0, :, pl.ds(pl.multiple_of(head * HD, HD), HD)]
        for first, count in BANDS:
            rows = rows_of(first, count)
            queries = queries_of(first, count)
            scores = dot(queries, keys2, ((1,), (1,)))
            scores = jnp.where(before > 0, scores, -1e30)
            old = stats[0, rows][:, :1]
            top = jnp.maximum(old, jnp.max(scores, axis=1, keepdims=True))
            weights = jnp.exp((scores - top) * SCALE)
            fade = jnp.exp((old - top) * SCALE)
            total = stats[1, rows][:, :1] * fade + jnp.sum(weights, axis=1, keepdims=True)
            result = acc[rows] * fade + dot(weights.astype(BF16), values2, ((1,), (0,)))
            result = (result * (1.0 / total)).reshape(2, 2 * count, ROWS, HD).astype(BF16)
            for y, slots in enumerate(slots_of(first, count)):
                osend[slots] = result[y]
            for i in range(4 * count):
                slot = i // 2 % 2 * HALF + 2 * (first + i // 4) + (i + 1) % 2

                @pl.when(slot != me)
                def _(slot=slot):
                    send("out", osend.at[slot], columns, (out_send, out_recv), (group, slot))

        out_ref[0, :, pl.ds(pl.multiple_of(head * HD, HD), HD)] = osend[me]

    @pl.when(is_head)
    def _():
        wait("out", out_ref.at[0, :, pl.ds(0, (HEADS - 1) * HD)], out_recv)

    @pl.when(jnp.logical_not(is_head))
    def _():
        wait("out", out_ref.at[0], out_recv)

    wait("part", others, part_send)

    @pl.when(is_head)
    def _():
        wait("own", pack.at[pl.ds(0, HEADS - 1)], own_send)
        wait("out", osend.at[pl.ds(0, SEQ - 1)], out_send)

    @pl.when(jnp.logical_not(is_head))
    def _():
        wait("own", pack, own_send)

    for count in (2 * GROUPS - 1, 2 * GROUPS, 3 * GROUPS - 1, 3 * GROUPS):

        @pl.when(sent == count)
        def _(count=count):
            left = prev.at[pl.ds(0, count)]
            wait("prev", left, prev_send)


def solution(mesh):
    def shards(queries, keys, values, span_index):
        return pl.pallas_call(
            kernel,
            out_shape=pltpu.VMEM((1, ROWS, HEADS * HD), BF16),
            in_specs=[pl.BlockSpec(memory_space=pl.ANY)] * 4,
            out_specs=pl.BlockSpec(memory_space=pltpu.VMEM),
            scratch_shapes=[
                pltpu.SMEM((GROUPS,), jnp.int32),
                pltpu.VMEM((3, ROWS, HEADS * HD), BF16),
                pltpu.VMEM((HEADS, 3, ROWS, HD), BF16),
                pltpu.VMEM((GROUPS, 3, 2, ROWS, HD), BF16),
                pltpu.VMEM((GROUPS, 3, 2, ROWS, HD), BF16),
                pltpu.VMEM((GROUPS, 3, 2, ROWS, HD), BF16),
                pltpu.VMEM((SEQ, 3, ROWS, HD), BF16),
                pltpu.VMEM((SEQ, 2, ROWS, HD), BF16),
                pltpu.VMEM((2, SEQ * ROWS, HD), F32),
                pltpu.VMEM((SEQ * ROWS, HD), F32),
                pltpu.VMEM((SEQ, ROWS, HD), BF16),
                pltpu.SemaphoreType.DMA((3,)),
            ]
            + [pltpu.SemaphoreType.DMA] * 9
            + [pltpu.SemaphoreType.REGULAR],
            compiler_params=pltpu.CompilerParams(
                collective_id=0, has_side_effects=True, vmem_limit_bytes=60 * 1024 * 1024
            ),
        )(span_index, queries, keys, values)

    in_specs = (P("span", "seq", None), P("span", "seq", None), P("span", "seq", None), P())
    return jax.shard_map(shards, mesh=mesh, in_specs=in_specs, out_specs=P("span", "seq", None), check_vma=False)
```
